32 devices in a mesh: groups: 2 (over x), tensor: 8 (over z, y), dp: 2 (over core).
Axes of the slice: x: 2, y: 2, z: 4, core: 2. Of those that a mesh axis runs over, the one named last changes fastest.
Arguments:
- tokens: bfloat16 [2048, 8192], P(('groups', 'dp'), 'tensor'), parts along dimension 0, may hold values from -6 to 6
- cotangent: bfloat16 [2048, 8192], P(('groups', 'dp'), 'tensor'), parts along dimension 0, may hold values from -6 to 6
- up_weight: bfloat16 [8192, 28672], P('dp', 'tensor'), may hold values from -0.0625 to 0.0625
- down_weight: bfloat16 [28672, 8192], P('tensor', 'dp'), may hold values from -0.03125 to 0.03125
- proj_inputs: bfloat16 [8192, 64], P('tensor'), may hold values from -0.0625 to 0.0625
- proj_hidden: bfloat16 [28672, 64], P('tensor'), may hold values from -0.03125 to 0.03125
- proj_hgrad: bfloat16 [28672, 64], P('tensor'), may hold values from -0.03125 to 0.03125
- proj_outgrad: bfloat16 [8192, 64], P('tensor'), may hold values from -0.0625 to 0.0625
- segment_ids: int32 [2048], P(('groups', 'dp')), parts along dimension 0, may hold values from 0 to 7, never falling along the last dimension, each value on 1 to 384 neighbouring positions
- queries: bfloat16 [512, 8192], P(('tensor', 'dp')), may hold values from -0.015625 to 0.015625
Outputs:
- scores: float32 [16, 512], P(('groups', 'dp'), 'tensor'), parts along dimension 0
The draws below stay inside these ranges and needn't reach their ends.
There are 2 independent parts, one for each index of `groups`. The reference program is written for one: setup_inputs(seed, part) draws one part's arguments, and reference() takes and returns one part's arrays. A program takes and returns all parts, laid end to end along the dimension named above; an argument that names none is the same for every part. Nothing has to cross between parts.
Inputs may be any that keep to these rules, and one draw needn't show every extreme that they name: `segment_ids`: Non-decreasing along the window; each of the 8 examples has 1 to 384 tokens and one has exactly 384.
All inputs are finite; a program needn't handle non-finite values.
Results may differ from the reference program's by a relative error of at most 0.0029.
Values may be sent and summed in bfloat16 or wider, within the bound.
A program may use at most 256 MiB of HBM per device.

```python
import math
import jax
import jax.numpy as jnp
import numpy as np
from jax import lax

D = 8192
FF = 28672
RANK = 64
TOKENS = 1024
EXAMPLES = 8
MOST = 384
QUERIES = 512
FEATS = 8192


def steps_of(stream_key, extent, pieces, low, largest):
    level = 1.0
    for dim, blocks in pieces:
        draws = jax.random.uniform(jax.random.fold_in(jax.random.fold_in(stream_key, 6), dim), (blocks,), jnp.float32, low / len(pieces), largest / len(pieces))
        level = level * jnp.repeat(jnp.exp(draws), extent[dim] // blocks).reshape((-1,) + (1,) * (len(extent) - 1 - dim))
    return level


def split_up(count, total, most, slope):
    portions = [(1 << 20) // math.isqrt(grade ** slope) + 1 for grade in range(2, count + 1)]
    spare, counts = total - most - (count - 1), [1] * (count - 1)
    while spare > 0:
        free = [i for i in range(count - 1) if counts[i] < most]
        whole, budget = sum([portions[i] for i in free]), spare
        for i in free:
            more = min(most - counts[i], max(1, budget * portions[i] // whole), spare)
            counts[i] = counts[i] + more
            spare = spare - more
    return np.array([most] + counts)


def uneven_parts(rng, number_of, total, most, lean):
    if number_of == 2:
        one = jax.random.randint(rng, (), max(1, total - most), min(most, total - 1) + 1)
        return jnp.stack([one, total - one])
    sizes = jnp.asarray(split_up(number_of, total, most, lean), jnp.int32)
    couples = (number_of - 1) // 2
    giver, receiver = sizes[1:1 + 2 * couples:2], sizes[2:2 + 2 * couples:2]
    slack = jnp.minimum(giver - 1, most - receiver)
    shifted = jax.random.randint(jax.random.fold_in(rng, 1), (couples,), 0, 1 << 20) % (slack + 1)
    sizes = sizes.at[1:1 + 2 * couples:2].set(giver - shifted).at[2:2 + 2 * couples:2].set(receiver + shifted)
    return sizes[jax.random.permutation(jax.random.fold_in(rng, 2), number_of)]


def scatter_about(own_key, shape, deviation, bound, pieces=(), kind=jnp.bfloat16):
    gain = steps_of(own_key, shape, pieces, -0.22, 0.18) if pieces else 1.0
    entries = jax.random.normal(own_key, shape, jnp.float32) * deviation * gain
    return jnp.minimum(jnp.maximum(entries, -bound), bound).astype(kind)


def setup_inputs(seed: int = 0, part: int = 0) -> dict:
    splits = jax.random.split(jax.random.key(seed), 11)
    part_keys = jax.random.split(jax.random.fold_in(splits[10], part), 11)
    tokens = scatter_about(part_keys[0], (TOKENS, D), 1.0, 6.0, ((0, 2), (1, 8)))
    cotangent = scatter_about(part_keys[1], (TOKENS, D), 1.0, 6.0, ((0, 2), (1, 8)))
    up_weight = scatter_about(splits[2], (D, FF), D ** -0.5, 0.0625, ((0, 2), (1, 8)))
    down_weight = scatter_about(splits[3], (FF, D), FF ** -0.5, 0.03125, ((0, 8), (1, 2)))
    proj_inputs = scatter_about(splits[4], (D, RANK), D ** -0.5, 0.0625, ((0, 8),))
    proj_hidden = scatter_about(splits[5], (FF, RANK), FF ** -0.5, 0.03125, ((0, 8),))
    proj_hgrad = scatter_about(splits[6], (FF, RANK), FF ** -0.5, 0.03125, ((0, 8),))
    proj_outgrad = scatter_about(splits[7], (D, RANK), D ** -0.5, 0.0625, ((0, 8),))
    segment_ids = jnp.searchsorted(jnp.cumsum(uneven_parts(part_keys[8], EXAMPLES, TOKENS, MOST, 2)), jnp.arange(TOKENS), side="right").astype(jnp.int32)
    queries = scatter_about(splits[9], (QUERIES, FEATS), (FEATS * 16) ** -0.5, 0.015625, ((0, 16),))
    return dict(tokens=tokens, cotangent=cotangent, up_weight=up_weight, down_weight=down_weight, proj_inputs=proj_inputs, proj_hidden=proj_hidden, proj_hgrad=proj_hgrad, proj_outgrad=proj_outgrad, segment_ids=segment_ids, queries=queries)


def example_grads(left, right, segment_ids):
    onehot = (segment_ids[:, None] == jnp.arange(EXAMPLES, dtype=jnp.int32)[None, :]).astype(jnp.float32)
    weighted = (onehot[:, :, None] * left[:, None, :]).reshape(left.shape[0], EXAMPLES * RANK)
    outer = lax.dot_general(weighted, right, (((0,), (0,)), ((), ())), precision=lax.Precision.HIGHEST, preferred_element_type=jnp.float32)
    return outer.reshape(EXAMPLES, RANK * RANK)


def reference(tokens, cotangent, up_weight, down_weight, proj_inputs, proj_hidden, proj_hgrad, proj_outgrad, segment_ids, queries):
    pre = jnp.dot(tokens, up_weight, preferred_element_type=jnp.float32)
    hidden = jax.nn.silu(pre).astype(jnp.bfloat16)
    back = lax.dot_general(cotangent, down_weight, (((1,), (1,)), ((), ())), preferred_element_type=jnp.float32)
    sig = jax.nn.sigmoid(pre)
    hgrad = (back * sig * (1.0 + pre * (1.0 - sig))).astype(jnp.bfloat16)
    in_up = jnp.dot(tokens, proj_inputs, preferred_element_type=jnp.float32)
    out_up = jnp.dot(hgrad, proj_hgrad, preferred_element_type=jnp.float32)
    in_down = jnp.dot(hidden, proj_hidden, preferred_element_type=jnp.float32)
    out_down = jnp.dot(cotangent, proj_outgrad, preferred_element_type=jnp.float32)
    grads = jnp.concatenate([example_grads(in_up, out_up, segment_ids), example_grads(in_down, out_down, segment_ids)], axis=1)
    return lax.dot_general(grads, queries.astype(jnp.float32), (((1,), (1,)), ((), ())), precision=lax.Precision.HIGHEST, preferred_element_type=jnp.float32)
```

```python
import functools

import jax
import jax.numpy as jnp
from jax import lax
from jax.experimental import pallas as pl
from jax.experimental.pallas import tpu as pltpu
from jax.sharding import PartitionSpec as P

MESH = pl.DeviceIdType.MESH
F32 = jnp.float32
BF16 = jnp.bfloat16
EX_DEV = 4
TILE = 512


def swapped(block, axis, bit):
    count = lax.axis_size(axis)
    route = []
    for low in range(count):
        high = low | 1 << bit
        if high != low and high < count:
            route += [(low, high), (high, low)]
    return lax.ppermute(block, axis, route)


def example_grads(left, right, segment_ids, count, rank):
    onehot = (segment_ids[:, None] == jnp.arange(count, dtype=jnp.int32)[None, :]).astype(
        jnp.float32
    )
    weighted = (onehot[:, :, None] * left[:, None, :]).reshape(left.shape[0], count * rank)
    outer = lax.dot_general(
        weighted,
        right,
        (((0,), (0,)), ((), ())),
        precision=lax.Precision.HIGHEST,
        preferred_element_type=jnp.float32,
    )
    return outer.reshape(count, rank * rank)


def contract_last(left, right):
    return lax.dot_general(
        left, right, (((1,), (1,)), ((), ())), preferred_element_type=jnp.float32
    )


def general(
    tokens,
    cotangent,
    up_weight,
    down_weight,
    proj_inputs,
    proj_hidden,
    proj_hgrad,
    proj_outgrad,
    segment_ids,
    queries,
):
    rank = proj_inputs.shape[1]
    part_in = jnp.dot(tokens, proj_inputs, preferred_element_type=jnp.float32)
    part_out = jnp.dot(cotangent, proj_outgrad, preferred_element_type=jnp.float32)
    full_x, full_dy = (
        lax.all_gather(tokens, "tensor", axis=1, tiled=True),
        lax.all_gather(cotangent, "tensor", axis=1, tiled=True),
    )
    half = up_weight.shape[0]
    side = lax.axis_index("dp")
    own_x = lax.dynamic_slice_in_dim(full_x, side * half, half, 1)
    own_dy = lax.dynamic_slice_in_dim(full_dy, side * half, half, 1)
    far_x = lax.dynamic_slice_in_dim(full_x, (1 - side) * half, half, 1)
    far_dy = lax.dynamic_slice_in_dim(full_dy, (1 - side) * half, half, 1)
    recv_x, recv_dy = swapped((far_x, far_dy), "dp", 0)
    lent_pre = jnp.dot(recv_x, up_weight, preferred_element_type=jnp.float32)
    lent_back = contract_last(recv_dy, down_weight)
    ret_pre, ret_back = swapped((lent_pre, lent_back), "dp", 0)
    pre = jnp.dot(own_x, up_weight, preferred_element_type=jnp.float32) + ret_pre
    back = contract_last(own_dy, down_weight) + ret_back
    hidden = jax.nn.silu(pre).astype(jnp.bfloat16)
    sig = jax.nn.sigmoid(pre)
    hgrad = (back * sig * (1.0 + pre * (1.0 - sig))).astype(jnp.bfloat16)
    part_hg = jnp.dot(hgrad, proj_hgrad, preferred_element_type=jnp.float32)
    part_hid = jnp.dot(hidden, proj_hidden, preferred_element_type=jnp.float32)
    stacked = jnp.concatenate([part_in, part_hg, part_hid, part_out], axis=1)
    factors = lax.psum(stacked, "tensor")
    count = EX_DEV * 2
    grads = jnp.concatenate(
        [
            example_grads(factors[:, :rank], factors[:, rank : 2 * rank], segment_ids, count, rank),
            example_grads(
                factors[:, 2 * rank : 3 * rank], factors[:, 3 * rank :], segment_ids, count, rank
            ),
        ],
        axis=1,
    )
    block = lax.all_gather(queries, "dp", axis=0, tiled=True).astype(jnp.float32)
    mine = lax.psum_scatter(grads, "dp", scatter_dimension=0, tiled=True)
    scores = lax.dot_general(
        mine,
        block,
        (((1,), (1,)), ((), ())),
        precision=lax.Precision.HIGHEST,
        preferred_element_type=jnp.float32,
    )
    return scores


def units(*names):
    return [(int(u[0]), 1 if u.endswith("'") else 0, "xd".index(u[1])) for u in names]


END = units("0x", "0d", "1x", "0x'", "1d", "0d'", "2x", "1x'", "2d", "1d'", "3x", "2x'", "3d", "2d'", "3x'", "3d'")
MID = units("1x", "1d", "2x", "0x", "2d", "0d", "1x'", "3x", "1d'", "3d", "2x'", "0x'", "2d'", "0d'", "3x'", "3d'")
END_NEAR = units("0x", "0d", "1x", "0x'", "1d", "0d'", "1x'", "1d'")
MID_NEAR = units("1x", "1d", "0x", "1x'", "0d", "1d'", "0x'", "0d'")
FAR = units("2x", "2d", "3x", "2x'", "3d", "2d'", "3x'", "3d'")
END_TO = {"0x": (0, 2), "0d": (0, 2), "1x": (2,), "1d": (2,), "2x": (2,), "2d": (2,), "3x": (2,), "0x'": (0,), "0d'": (0,)}
MID_TO = {"1x": (0, 1, 2), "1d": (0, 1, 2), "2x": (0, 2), "2d": (0, 2), "3x": (0, 2), "3d": (0, 2), "0x": (1,), "0d": (1,), "3d'": (0,)}
END_SENDS = {units(u)[0]: to for u, to in END_TO.items()}
MID_SENDS = {units(u)[0]: to for u, to in MID_TO.items()}


def kernel(
    tok, cot, up, down, pin, phid, phg, pout, qry,
    in_up, out_up, in_down, out_down, up_far, down_far, q_far,
    held, pre, back, wbuf, part, land, full,
    own_sem, w_sem, send_sem, recv_sem, hs_sem, hr_sem, ws_sem, wr_sem, fs_sem, fr_sem,
):
    rows, feats = tok.shape
    tiles = pre.shape[0]
    n = full.shape[1]
    me = lax.axis_index("tensor")
    d = lax.axis_index("dp")
    z, y = me // 2, me % 2
    s = z // 2
    is_end = (z == 0) | (z == 3)
    is_mid = jnp.logical_not(is_end)

    def place(m):
        return m + s * (3 - 2 * m)

    def source(unit):
        m, row, _ = unit
        return place(m) * 2 + (y if row == 0 else 1 - y)

    def either(a, b):
        return jnp.where(is_end, a, b)

    nbr = (either(place(1), place(0)) * 2 + y, place(2) * 2 + y, z * 2 + 1 - y)

    barrier = pltpu.get_barrier_semaphore()
    for k in range(1, n):
        pl.semaphore_signal(barrier, inc=1, device_id={"tensor": lax.rem(me + k, n)}, device_id_type=MESH)
    pl.semaphore_signal(barrier, inc=1, device_id={"dp": 1 - d}, device_id_type=MESH)

    mine = [
        pltpu.make_async_copy(tok, held.at[me * 2], own_sem.at[0]),
        pltpu.make_async_copy(cot, held.at[me * 2 + 1], own_sem.at[1]),
    ]
    for c in mine:
        c.start()
    pl.semaphore_wait(barrier, n)

    def in_halves(link, unit):
        return unit[0] == 3 and (link == 2 or unit[1] == 1)

    def send_half(link, unit, h):
        slot = source(unit) * 2 + unit[2]
        part_of = pl.ds(h * (rows // 2), rows // 2)
        return pltpu.make_async_remote_copy(
            src_ref=held.at[slot, part_of], dst_ref=held.at[slot, part_of],
            send_sem=hs_sem.at[unit[2], unit[1], h], recv_sem=hr_sem.at[unit[2], h],
            device_id={"tensor": nbr[link]}, device_id_type=MESH,
        )

    def send(link, unit):
        slot = source(unit) * 2 + unit[2]
        return pltpu.make_async_remote_copy(
            src_ref=held.at[slot], dst_ref=held.at[slot],
            send_sem=send_sem.at[link, slot], recv_sem=recv_sem.at[slot],
            device_id={"tensor": nbr[link]}, device_id_type=MESH,
        )

    def copies(link, unit):
        if in_halves(link, unit):
            return [send_half(link, unit, h) for h in range(2)]
        return [send(link, unit)]

    def forward(step):
        for role, order, sends in ((is_end, END, END_SENDS), (is_mid, MID, MID_SENDS)):
            links = sends.get(order[step], ())
            if links:
                @pl.when(role)
                def _():
                    for link in links:
                        for c in copies(link, order[step]):
                            c.start()

    def slot_of(step):
        return either(source(END[step]), source(MID[step])) * 2 + END[step][2]

    def block(near, far, kind, src):
        at = pl.ds(pl.multiple_of((src % 4) * feats, feats), feats)
        return (near.at[at], far.at[at]) if kind == 0 else (near.at[:, at], far.at[:, at])

    def lend(kind, src):
        here, there = block(up, up_far, 0, src) if kind == 0 else block(down, down_far, 1, src)
        return pltpu.make_async_remote_copy(
            src_ref=here, dst_ref=there,
            send_sem=ws_sem.at[kind, src % 4], recv_sem=wr_sem.at[kind, src % 4],
            device_id={"dp": 1 - d}, device_id_type=MESH,
        )

    lent = []
    for k in range(8):
        near = either(source(END_NEAR[k]), source(MID_NEAR[k]))
        lent.append((FAR[k][2], jnp.where(s == d, near, source(FAR[k]))))

    q_copy = pltpu.make_async_remote_copy(
        src_ref=qry, dst_ref=q_far, send_sem=own_sem.at[2], recv_sem=own_sem.at[3],
        device_id={"dp": 1 - d}, device_id_type=MESH,
    )

    for step in range(2):
        mine[step].wait()
        forward(step)
    for kind, src in lent:
        lend(kind, src).start()
    q_copy.start()

    def load(step):
        kind, b = END[step][2], step % 2
        src = slot_of(step) // 2

        def tiles_from(w):
            at = pl.multiple_of((src % 4) * feats, feats)

            def body(i, carry):
                cols = pl.ds(pl.multiple_of(i * TILE, TILE), TILE)
                if kind == 0:
                    pltpu.make_async_copy(w.at[pl.ds(at, feats), cols], wbuf.at[b, i], w_sem.at[b]).start()
                else:
                    for h in range(feats // TILE):
                        pltpu.make_async_copy(
                            w.at[cols, pl.ds(at + h * TILE, TILE)],
                            wbuf.at[b, i, pl.ds(h * TILE, TILE)], w_sem.at[b],
                        ).start()
                return carry

            lax.fori_loop(0, tiles, body, 0)

        @pl.when(src // 4 == d)
        def _():
            tiles_from((up, down)[kind])

        @pl.when(src // 4 != d)
        def _():
            lend(kind, src).wait_recv()
            tiles_from((up_far, down_far)[kind])

    def product(kind, slot, b, i, at=slice(None)):
        a = held[slot, at]
        if kind == 0:
            return jnp.dot(a, wbuf[b, i], preferred_element_type=F32)
        out = None
        for h in range(feats // TILE):
            p = lax.dot_general(
                a[:, h * TILE:(h + 1) * TILE], wbuf[b, i, h * TILE:(h + 1) * TILE],
                (((1,), (1,)), ((), ())), preferred_element_type=F32,
            )
            out = p if out is None else out + p
        return out

    def peer_copy(g, phase, k):
        peer = lax.rem(me + k, n)
        src, dst = (part.at[g, peer], land.at[g, me]) if phase == 0 else (full.at[g, me], full.at[g, me])
        return pltpu.make_async_remote_copy(
            src_ref=src, dst_ref=dst, send_sem=fs_sem.at[g, phase, peer], recv_sem=fr_sem.at[g, phase, me],
            device_id={"tensor": peer}, device_id_type=MESH,
        )

    def arrived(g, phase, k):
        peer = lax.rem(me + k, n)
        ref = land.at[g, peer] if phase == 0 else full.at[g, peer]
        pltpu.make_async_remote_copy(
            src_ref=ref, dst_ref=ref, send_sem=fs_sem.at[g, phase, peer], recv_sem=fr_sem.at[g, phase, peer],
            device_id={"tensor": peer}, device_id_type=MESH,
        ).wait_recv()

    def start_all(g, phase):
        for k in range(1, n):
            peer_copy(g, phase, k).start()

    def add_up(g):
        total = part[g, me]
        for k in range(1, n):
            arrived(g, 0, k)
            total = total + land[g, lax.rem(me + k, n)]
        full[g, me] = total
        start_all(g, 1)

    def keep(g, col, value, first=0):
        r = rows // n
        w = value.shape[1]
        for k in range(value.shape[0] // r):
            part[g, first + k, :, col * w:(col + 1) * w] = value[k * r:(k + 1) * r]

    load(0)
    for step in range(14):
        kind, b = END[step][2], step % 2
        slot = slot_of(step)
        if step >= 2:
            pltpu.make_async_copy(held.at[slot], held.at[slot], recv_sem.at[slot]).wait()
            forward(step)
        pltpu.make_async_copy(wbuf.at[b], wbuf.at[b], w_sem.at[b]).wait()
        load(step + 1)
        acc = (pre, back)[kind]
        if step == 0:
            keep(0, 0, contract_last(held[slot], pin[...]))
        if step == 1:
            keep(0, 1, contract_last(held[slot], pout[...]))
            start_all(0, 0)
        if step == 8:
            add_up(0)
        if step < 2:
            def body(i, carry):
                acc[i] = product(kind, slot, b, i)
                return carry
            lax.fori_loop(0, tiles, body, 0)
        else:
            def body(i, carry):
                acc[i] += product(kind, slot, b, i)
                return carry
            lax.fori_loop(0, tiles, body, 0)
    load(15)
    half = rows // 2
    for h in range(2):
        at = slice(h * half, (h + 1) * half)
        for kind in range(2):
            slot = slot_of(14 + kind)
            there = held.at[slot, pl.ds(h * half, half)]
            pltpu.make_async_copy(there, there, hr_sem.at[kind, h]).wait()
            if kind == 1:
                @pl.when(is_mid)
                def _():
                    send_half(0, MID[15], h).start()
            if h == 0:
                pltpu.make_async_copy(wbuf.at[kind], wbuf.at[kind], w_sem.at[kind]).wait()
            weight = (phid, phg)[kind]

            def body(i, total):
                cols = pl.ds(pl.multiple_of(i * TILE, TILE), TILE)
                v = (pre, back)[kind][i, at] + product(kind, slot, kind, i, at)
                if kind == 0:
                    sig = jax.nn.sigmoid(v)
                    pre[i, at] = sig * (1.0 + v * (1.0 - sig))
                    u = v * sig
                else:
                    u = v * pre[i, at]
                return total + contract_last(u.astype(BF16), weight[:, cols])

            total = lax.fori_loop(0, tiles, body, jnp.zeros((half, weight.shape[0]), F32))
            keep(1, 1 - kind, total, h * (n // 2))
    start_all(1, 0)
    add_up(1)
    for k in range(1, n):
        arrived(0, 1, k)
    rank = in_up.shape[2]
    in_up[...] = full[0, :, :, :rank]
    out_down[...] = full[0, :, :, rank:]
    for k in range(1, n):
        arrived(1, 1, k)
    out_up[...] = full[1, :, :, :rank]
    in_down[...] = full[1, :, :, rank:]
    for g in range(2):
        for phase in range(2):
            for k in range(1, n):
                peer_copy(g, phase, k).wait_send()
    for role, sends in ((is_end, END_SENDS), (is_mid, MID_SENDS)):
        @pl.when(role)
        def _():
            for unit, links in sends.items():
                for link in links:
                    for c in copies(link, unit):
                        c.wait_send()
    for kind, src in lent:
        lend(kind, src).wait_send()
    q_copy.wait()


def fused(
    tokens, cotangent, up_weight, down_weight, proj_inputs, proj_hidden, proj_hgrad, proj_outgrad, segment_ids, queries,
):
    rows, feats = tokens.shape
    width = up_weight.shape[1]
    rank = proj_inputs.shape[1]
    n = lax.axis_size("tensor")
    tiles = width // TILE
    hbm = pl.BlockSpec(memory_space=pl.ANY)
    vmem = pl.BlockSpec(memory_space=pltpu.VMEM)
    shape = jax.ShapeDtypeStruct
    dma = pltpu.SemaphoreType.DMA
    *factors, _, _, q_far = pl.pallas_call(
        kernel,
        out_shape=(
            *[shape((n, rows // n, rank), F32)] * 4,
            shape(up_weight.shape, BF16), shape(down_weight.shape, BF16), shape(queries.shape, BF16),
        ),
        in_specs=[hbm, hbm, hbm, hbm, vmem, vmem, vmem, vmem, hbm],
        out_specs=(vmem, vmem, vmem, vmem, hbm, hbm, hbm),
        scratch_shapes=[
            pltpu.VMEM((2 * n, rows, feats), BF16),
            pltpu.VMEM((tiles, rows, TILE), F32),
            pltpu.VMEM((tiles, rows, TILE), F32),
            pltpu.VMEM((2, tiles, feats, TILE), BF16),
            pltpu.VMEM((2, n, rows // n, 2 * rank), F32),
            pltpu.VMEM((2, n, rows // n, 2 * rank), F32),
            pltpu.VMEM((2, n, rows // n, 2 * rank), F32),
            dma((4,)), dma((2,)), dma((3, 2 * n)), dma((2 * n,)), dma((2, 2, 2)), dma((2, 2)),
            dma((2, 4)), dma((2, 4)), dma((2, 2, n)), dma((2, 2, n)),
        ],
        compiler_params=pltpu.CompilerParams(collective_id=0, has_side_effects=True, vmem_limit_bytes=60 << 20),
    )(
        tokens, cotangent, up_weight, down_weight, proj_inputs.T,
        proj_hidden.T, proj_hgrad.T, proj_outgrad.T, queries,
    )
    in_up, out_up, in_down, out_down = [f.reshape(rows, rank) for f in factors]
    grads = jnp.concatenate(
        [
            example_grads(in_up, out_up, segment_ids, 2 * EX_DEV, rank),
            example_grads(in_down, out_down, segment_ids, 2 * EX_DEV, rank),
        ],
        axis=1,
    )
    d = lax.axis_index("dp")
    block = jnp.where(d == 0, jnp.concatenate([queries, q_far]), jnp.concatenate([q_far, queries])).astype(F32)
    scores = lax.dot_general(
        grads, block, (((1,), (1,)), ((), ())), precision=lax.Precision.HIGHEST, preferred_element_type=F32
    )
    far = lax.dynamic_slice_in_dim(scores, (1 - d) * EX_DEV, EX_DEV, 0)
    own = lax.dynamic_slice_in_dim(scores, d * EX_DEV, EX_DEV, 0)
    return own + swapped(far, "dp", 0)


def solution(mesh):
    placed = (
        P(("groups", "dp"), "tensor"),
        P(("groups", "dp"), "tensor"),
        P("dp", "tensor"),
        P("tensor", "dp"),
        P("tensor", None),
        P("tensor", None),
        P("tensor", None),
        P("tensor", None),
        P(("groups", "dp")),
        P(("tensor", "dp"), None),
    )
    fits = mesh.shape["tensor"] == 8 and mesh.shape["dp"] == 2
    return jax.shard_map(
        fused if fits else general, mesh=mesh, in_specs=placed, out_specs=P(("groups", "dp"), "tensor"), check_vma=False
    )
```
